32 devices in a mesh: dp: 16 (over z, y, x), tensor: 2 (over core).
Axes of the slice: x: 2, y: 2, z: 4, core: 2. Of those that a mesh axis runs over, the one named last changes fastest.
Arguments:
- tokens: bfloat16 [2048, 768], P('dp'), may hold values from -6 to 6
- cotangent: bfloat16 [2048, 768], P('dp'), may hold values from -6 to 6
- seq_lengths: int32 [32], replicated, may hold values from 16 to 112, as said below
- seq_owner: int32 [32], replicated, may hold values from 0 to 15, as said below
- routes: int32 [2048, 1], P('dp'), may hold values from 0 to 3; in each aligned block of 128 rows (0 to 127, 128 to 255, ...) at most 42 rows name the same one
- rel_buckets: int32 [255], replicated, may hold values from 0 to 31
- attn_gain: float32 [768], replicated, may hold values from 0.5 to 1.5
- query_weight: bfloat16 [768, 768], P(None, 'tensor'), may hold values from -0.02734375 to 0.02734375
- key_weight: bfloat16 [768, 768], P(None, 'tensor'), may hold values from -0.21875 to 0.21875
- value_weight: bfloat16 [768, 768], P(None, 'tensor'), may hold values from -0.21875 to 0.21875
- output_weight: bfloat16 [768, 768], P('tensor'), may hold values from -1.75 to 1.75
- bias_table: float32 [32, 12], P(None, 'tensor'), may hold values from -4 to 4
- ffn_gain: float32 [768], replicated, may hold values from 0.5 to 1.5
- router_weight: bfloat16 [768, 4], replicated, may hold values from -0.15625 to 0.15625
- expert_in: bfloat16 [768, 12288], P(None, ('dp', 'tensor')), may hold values from -0.21875 to 0.21875
- expert_out: bfloat16 [12288, 768], P(('dp', 'tensor')), may hold values from -1.75 to 1.75
Outputs:
- output: bfloat16 [2048, 768], P('dp')
- tokens_grad: bfloat16 [2048, 768], P('dp')
- attn_gain_grad: float32 [768], replicated
- query_grad: float32 [768, 768], P(None, 'tensor')
- key_grad: float32 [768, 768], P(None, 'tensor')
- value_grad: float32 [768, 768], P(None, 'tensor')
- output_weight_grad: float32 [768, 768], P('tensor')
- table_grad: float32 [32, 12], P(None, 'tensor')
- ffn_gain_grad: float32 [768], replicated
- router_grad: float32 [768, 4], replicated
- expert_in_grad: float32 [768, 12288], P(None, ('dp', 'tensor'))
- expert_out_grad: float32 [12288, 768], P(('dp', 'tensor'))
The draws below stay inside these ranges and needn't reach their ends.
Inputs may be any that keep to these rules, and one draw needn't show every extreme that they name: `seq_lengths`: each index of dp owns exactly two sequences, 2i and 2i + 1 for some i, whose lengths add up to 64 to 128; the two of some index add up to exactly 128. `seq_owner`: sequences 2i and 2i + 1 have the same owner, and every index of dp owns one such pair. `routes`: among the rows of one index of dp at most 42 name any one expert.
All inputs are finite; a program needn't handle non-finite values.
Results may differ from the reference program's by a relative error of at most 0.018.
Values may be sent and summed in bfloat16 or wider, within the bound.
A program may use at most 128 MiB of HBM per device.

```python
import math
from functools import partial
import jax
import jax.numpy as jnp
import numpy as np
from jax import lax

D = 768
HEADS = 12
HEAD_DIM = 64
FF = 3072
BUCKETS = 32
TOK_DEV = 128
SEQ_MIN = 16
EXPERTS = 4
CAP = 42
SEQS = 32
TOKENS = 2048
N_DP = 16


def deal_sequences(key):
    pairs = SEQS // 2
    total_key, split_key, order_key = jax.random.split(key, 3)
    totals = jax.random.randint(total_key, (pairs,), TOK_DEV // 2, TOK_DEV + 1)
    totals = totals.at[0].set(TOK_DEV)
    first = jax.random.randint(split_key, (pairs,), SEQ_MIN, totals - SEQ_MIN + 1)
    first = first.at[0].set(TOK_DEV - SEQ_MIN)
    lengths = jnp.stack([first, totals - first], axis=1).reshape(SEQS)
    owners = jnp.repeat(jax.random.permutation(order_key, pairs), 2)
    return (lengths.astype(jnp.int32), owners.astype(jnp.int32))


def draw_seq_lengths(key, part):
    return deal_sequences(key)[0]


def draw_seq_owner(key, part):
    return deal_sequences(key)[1]


def touch_ends(entries, own_key, smallest, high):
    spot = [jax.random.randint(jax.random.fold_in(own_key, axis), (), 0, length) for axis, length in enumerate(entries.shape)]
    longest = entries.shape.index(max(entries.shape))
    next_to = spot[:longest] + [(spot[longest] + 1) % entries.shape[longest]] + spot[longest + 1:]
    return entries.at[tuple(spot)].set(smallest).at[tuple(next_to)].set(high)


def level_of(key, dims, pieces, low, high):
    level, own = 1.0, jax.random.fold_in(key, 6)
    for dim, parts in pieces:
        draws = jnp.exp(jax.random.uniform(jax.random.fold_in(own, dim), (parts,), jnp.float32, low / len(pieces), high / len(pieces)))
        level = level * jnp.repeat(draws, dims[dim] // parts).reshape([-1 if axis == dim else 1 for axis in range(len(dims))])
    return level


def deal_out(stream_key, own, number, rows, amount, top, reach, lean):
    order = jax.random.permutation(stream_key, amount)
    packed, ordinary = portions_of(amount, rows * top, reach, lean, True), portions_of(amount, rows * top, reach, lean, False)
    places = jnp.arange(amount)

    def named(tallies, rotation):
        used = int((tallies > 0).sum())
        fixed = max(1, used // 4)
        shifted = fixed + (places - fixed + rotation * (used - fixed)) % max(1, amount - fixed)
        return jnp.zeros((amount,), jnp.int32).at[order[jnp.where(places < fixed, places, shifted)]].set(jnp.asarray(tallies, jnp.int32))

    tallies = jnp.where(number % 4 == 0, named(packed, number // 4), named(ordinary, number - number // 4 - 1))
    mixed = jax.random.permutation(jax.random.fold_in(own, 3), amount)
    donor, receiver = mixed[0:amount // 2 * 2:2], mixed[1:amount // 2 * 2:2]
    slack = jnp.minimum(tallies[donor] - 1, reach - tallies[receiver]) // 2
    slack = jnp.where((donor == order[0]) | (receiver == order[0]) | (tallies[receiver] == 0), 0, jnp.maximum(slack, 0))
    shifted = jax.random.randint(jax.random.fold_in(own, 4), (amount // 2,), 0, 1 << 20) % (slack + 1)
    tallies = tallies.at[donor].add(-shifted).at[receiver].add(shifted)
    members = jnp.searchsorted(jnp.cumsum(tallies), jnp.arange(rows * top), side="right").astype(jnp.int32)
    listing = members.reshape(top, rows).T
    listing = listing[jax.random.permutation(jax.random.fold_in(own, 1), rows)]
    rotation = jax.random.randint(jax.random.fold_in(own, 2), (rows, 1), 0, top)
    return jnp.take_along_axis(listing, (jnp.arange(top)[None, :] + rotation) % top, axis=1)


def portions_of(amount, total, limit, skew, full):
    loads = [(1 << 20) // math.isqrt(grade ** skew) + 1 for grade in range(1, amount + 1)]
    largest = limit if full else min(limit, max(-(-total // amount), total * loads[0] // sum(loads)))
    least = 1 if total - largest >= amount - 1 else 0
    holding, spare = [largest] + [least] * (amount - 1), total - largest - least * (amount - 1)
    while spare > 0:
        candidates = [i for i in range(1, amount) if holding[i] < largest] or [i for i in range(1, amount) if holding[i] < limit]
        mass, left = sum([loads[i] for i in candidates]), spare
        for i in candidates:
            addition = min(limit - holding[i], max(1, left * loads[i] // mass), spare)
            holding[i] = holding[i] + addition
            spare = spare - addition
    return np.array(holding)


def gaussian(stream_key, extent, scale, limit, pieces=(), kind=jnp.bfloat16):
    drawn = jax.random.normal(stream_key, extent, jnp.float32) * scale
    if len(pieces) > 0:
        drawn = level_of(stream_key, extent, pieces, -0.22, 0.18) * drawn
    return jnp.clip(drawn, min=-limit, max=limit).astype(kind)


def setup_inputs(seed: int = 0) -> dict:
    arg_keys = jax.random.split(jax.random.key(seed), 17)
    tokens = gaussian(arg_keys[0], (TOKENS, D), 1.0, 6.0, ((0, 16),))
    cotangent = gaussian(arg_keys[1], (TOKENS, D), 1.0, 6.0, ((0, 16),))
    seq_lengths = draw_seq_lengths(jax.random.fold_in(arg_keys[16], 71), 0)
    seq_owner = draw_seq_owner(jax.random.fold_in(arg_keys[16], 71), 0)
    routes_keys = jax.random.split(jax.random.fold_in(arg_keys[4], 1), TOKENS // TOK_DEV)
    routes_turns = jax.random.permutation(jax.random.fold_in(arg_keys[4], 3), TOKENS // TOK_DEV)
    routes = jax.vmap(lambda own, number: deal_out(jax.random.fold_in(arg_keys[4], 2), own, number, TOK_DEV, EXPERTS, 1, CAP, 2))(routes_keys, routes_turns).reshape((TOKENS, 1))
    rel_buckets = touch_ends(jax.random.randint(arg_keys[5], (2 * TOK_DEV - 1,), 0, BUCKETS), jax.random.fold_in(arg_keys[5], 1), 0, BUCKETS - 1).astype(jnp.int32)
    attn_gain = jnp.clip(1.0 + 0.1 * jax.random.normal(arg_keys[6], (D,), jnp.float32), 0.5, 1.5)
    query_weight = gaussian(arg_keys[7], (D, HEADS * HEAD_DIM), (64 * D) ** -0.5, 0.02734375, ((1, 2),))
    key_weight = gaussian(arg_keys[8], (D, HEADS * HEAD_DIM), D ** -0.5, 0.21875, ((1, 2),))
    value_weight = gaussian(arg_keys[9], (D, HEADS * HEAD_DIM), D ** -0.5, 0.21875, ((1, 2),))
    output_weight = gaussian(arg_keys[10], (HEADS * HEAD_DIM, D), (max(1, HEADS * HEAD_DIM // 64)) ** -0.5, 1.75, ((0, 2),))
    bias_table = gaussian(arg_keys[11], (BUCKETS, HEADS), 1.0, 4.0, ((1, 2),), jnp.float32)
    ffn_gain = jnp.clip(1.0 + 0.1 * jax.random.normal(arg_keys[12], (D,), jnp.float32), 0.5, 1.5)
    router_weight = gaussian(arg_keys[13], (D, EXPERTS), (2 * D) ** -0.5, 0.15625)
    expert_in = gaussian(arg_keys[14], (D, EXPERTS * FF), D ** -0.5, 0.21875, ((1, 32),))
    expert_out = gaussian(arg_keys[15], (EXPERTS * FF, D), (0.028 * EXPERTS), 1.75, ((0, 32),))
    return {"tokens": tokens, "cotangent": cotangent, "seq_lengths": seq_lengths, "seq_owner": seq_owner, "routes": routes, "rel_buckets": rel_buckets, "attn_gain": attn_gain, "query_weight": query_weight, "key_weight": key_weight, "value_weight": value_weight, "output_weight": output_weight, "bias_table": bias_table, "ffn_gain": ffn_gain, "router_weight": router_weight, "expert_in": expert_in, "expert_out": expert_out}


epsilon = 1e-06
highest = lax.Precision.HIGHEST

@jax.custom_vjp
def low(v):
    return lax.optimization_barrier(v.astype(jnp.bfloat16)).astype(jnp.float32)

@jax.custom_vjp
def low_back(v):
    return v

def low_keep(v):
    return (low(v), None)

def low_pass(kept, grad):
    return (grad,)

def back_keep(v):
    return (v, None)

def back_low(kept, grad):
    return (low(grad),)
low.defvjp(low_keep, low_pass)
low_back.defvjp(back_keep, back_low)

def rms_rows(rows, gain):
    return rows * lax.rsqrt(lax.optimization_barrier(jnp.mean(rows * rows, axis=-1, keepdims=True)) + epsilon) * gain

def layout(seq_lengths, seq_owner):
    blocks = jnp.arange(N_DP, dtype=jnp.int32)
    mine = (seq_owner[None, :] == blocks[:, None]).astype(jnp.int32)
    owned = mine * seq_lengths[None, :]
    starts = jnp.cumsum(owned, axis=1) - owned
    slots = jnp.arange(TOK_DEV, dtype=jnp.int32)
    inside = ((mine[:, :, None] > 0) & (slots[None, None, :] >= starts[:, :, None]) & (slots[None, None, :] < (starts + owned)[:, :, None])).astype(jnp.int32)
    count = lax.optimization_barrier(jnp.sum(inside, axis=1))
    numbers = jnp.arange(SEQS, dtype=jnp.int32)
    segment = lax.optimization_barrier(jnp.sum(inside * numbers[None, :, None], axis=1))
    return (jnp.where(count > 0, segment, -1), count > 0)

def attend_block(bias, block):
    queries, keys, values, segment = block
    positions = jnp.arange(TOK_DEV, dtype=jnp.int32)
    allowed = (segment[:, None] == segment[None, :]) & (segment[:, None] >= 0) | (positions[:, None] == positions[None, :])
    scores = low_back(jnp.einsum('ihc,jhc->hij', queries, keys, precision=highest) + bias)
    scores = jnp.where(allowed[None], scores, -1e+30)
    top = lax.optimization_barrier(jnp.max(scores, axis=-1, keepdims=True))
    weights = jnp.exp(scores - top)
    probs = low(weights / lax.optimization_barrier(jnp.sum(weights, axis=-1, keepdims=True)))
    return jnp.einsum('hij,jhc->ihc', probs, values, precision=highest)

def expert_apply(block):
    rows, first, second = block
    pre = low_back(jnp.dot(rows, first, precision=highest))
    act = low(jax.nn.gelu(pre))
    return jnp.dot(act, second, precision=highest)

def reference(tokens, cotangent, seq_lengths, seq_owner, routes, rel_buckets, attn_gain, query_weight, key_weight, value_weight, output_weight, bias_table, ffn_gain, router_weight, expert_in, expert_out):
    segment, valid = layout(seq_lengths, seq_owner)
    flat_valid = valid.reshape(TOKENS)
    keep = flat_valid.astype(jnp.float32)
    chosen = routes[:, 0]
    expert_ids = jnp.arange(EXPERTS, dtype=jnp.int32)
    picked = ((chosen[:, None] == expert_ids[None, :]) & flat_valid[:, None]).astype(jnp.int32)
    picked = picked.reshape(N_DP, TOK_DEV, EXPERTS)
    rank = lax.optimization_barrier(jnp.sum((jnp.cumsum(picked, axis=1) - picked) * picked, axis=2)).reshape(TOKENS)
    block_of = jnp.arange(TOKENS, dtype=jnp.int32) // TOK_DEV
    flat_slot = jnp.where(flat_valid, chosen * (N_DP * CAP) + block_of * CAP + rank, EXPERTS * N_DP * CAP).astype(jnp.int32)
    positions = jnp.arange(TOK_DEV, dtype=jnp.int32)
    offsets = positions[None, :] - positions[:, None] + TOK_DEV - 1
    bucket_grid = rel_buckets[offsets]
    route_hot = (chosen[:, None] == expert_ids[None, :]).astype(jnp.float32)

    def forward(inputs, gain_one, w_query, w_key, w_value, w_output, table, gain_two, w_router, w_first, w_second):
        normed = low(rms_rows(inputs, gain_one))

        def project(weight):
            return low(low_back(jnp.dot(normed, weight, precision=highest))).reshape(N_DP, TOK_DEV, HEADS, HEAD_DIM)
        bias = jnp.transpose(table[bucket_grid], (2, 0, 1))
        mixed = lax.map(jax.checkpoint(partial(attend_block, bias)), (project(w_query), project(w_key), project(w_value), segment))
        mixed = low(low_back(mixed.reshape(TOKENS, HEADS * HEAD_DIM)))
        attended = low_back(jnp.dot(mixed, w_output, precision=highest)) * keep[:, None]
        middle = inputs + attended
        normed_two = low(rms_rows(middle, gain_two))
        logits = low_back(jnp.dot(normed_two, w_router, precision=highest))
        gate = lax.optimization_barrier(jnp.sum(jax.nn.softmax(logits, axis=-1) * route_hot, axis=-1))
        buffer = jnp.zeros((EXPERTS * N_DP * CAP, D), jnp.float32).at[flat_slot].set(normed_two, mode='drop')
        first = jnp.transpose(w_first.reshape(D, EXPERTS, FF), (1, 0, 2))
        second = w_second.reshape(EXPERTS, FF, D)
        results = lax.map(jax.checkpoint(expert_apply), (buffer.reshape(EXPERTS, N_DP * CAP, D), first, second))
        expert_rows = low_back(jnp.take(results.reshape(EXPERTS * N_DP * CAP, D), flat_slot, axis=0, mode='fill', fill_value=0.0))
        return middle + gate[:, None] * expert_rows
    floats = (tokens.astype(jnp.float32), attn_gain.astype(jnp.float32), query_weight.astype(jnp.float32), key_weight.astype(jnp.float32), value_weight.astype(jnp.float32), output_weight.astype(jnp.float32), bias_table.astype(jnp.float32), ffn_gain.astype(jnp.float32), router_weight.astype(jnp.float32), expert_in.astype(jnp.float32), expert_out.astype(jnp.float32))
    result, pullback = jax.vjp(forward, *floats)
    grads = pullback(cotangent.astype(jnp.float32))
    return (result.astype(jnp.bfloat16), grads[0].astype(jnp.bfloat16), grads[1], grads[2], grads[3], grads[4], grads[5], grads[6], grads[7], grads[8], grads[9], grads[10])
```

```python
import functools

import jax
import jax.numpy as jnp
from jax import lax
from jax.experimental import pallas as pl
from jax.experimental.pallas import tpu as pltpu
from jax.sharding import PartitionSpec as P

HEAD_DIM = 64


epsilon = 1e-06


def rms_rows(rows, gain):
    scale = lax.rsqrt(jnp.mean(rows * rows, axis=-1, keepdims=True) + epsilon)
    return (rows * scale * gain, scale)


def rms_back(rows, gain, scale, grad):
    gain_grad = jnp.sum(grad * rows * scale, axis=0)
    inner = jnp.mean(rows * gain * grad, axis=-1, keepdims=True)
    return (scale * (gain * grad) - rows * (scale * scale * scale) * inner, gain_grad)


def block_layout(seq_lengths, seq_owner, rows):
    device = lax.axis_index("dp")
    mine = (seq_owner == device).astype(jnp.int32)
    owned = mine * seq_lengths
    order = jnp.arange(owned.shape[0], dtype=jnp.int32)
    starts = jnp.sum(jnp.where(order[None, :] < order[:, None], owned[None, :], 0), axis=1)
    slots = jnp.arange(rows, dtype=jnp.int32)
    inside = (
        (mine[:, None] > 0)
        & (slots[None, :] >= starts[:, None])
        & (slots[None, :] < (starts + owned)[:, None])
    ).astype(jnp.int32)
    count = jnp.sum(inside, axis=0)
    numbers = jnp.arange(seq_lengths.shape[0], dtype=jnp.int32)
    segment = jnp.sum(inside * numbers[:, None], axis=0)
    return (jnp.where(count > 0, segment, -1), count > 0)


def diagonal_sums(square):
    heads = square.shape[0]
    length = square.shape[1]
    flipped = square[:, ::-1, :]
    padded = jnp.pad(flipped, ((0, 0), (0, 0), (0, length)))
    flat = padded.reshape(heads, 2 * length * length)[:, : length * (2 * length - 1)]
    return jnp.sum(flat.reshape(heads, length, 2 * length - 1), axis=1)


MESH = pl.DeviceIdType.MESH
LIMIT = 48 * 1024 * 1024


def params(number):
    return pltpu.CompilerParams(
        collective_id=number, has_side_effects=True, vmem_limit_bytes=LIMIT
    )


def in_vmem(count):
    return [pl.BlockSpec(memory_space=pltpu.VMEM)] * count


def greet(peers):
    barrier = pltpu.get_barrier_semaphore()
    for peer in peers:
        pl.semaphore_signal(barrier, inc=1, device_id=peer, device_id_type=MESH)
    pl.semaphore_wait(barrier, len(peers))


def remote(src, dst, send_sem, recv_sem, peer):
    return pltpu.make_async_remote_copy(
        src_ref=src,
        dst_ref=dst,
        send_sem=send_sem,
        recv_sem=recv_sem,
        device_id=peer,
        device_id_type=MESH,
    )


def place(quarter):
    device = lax.axis_index("dp")
    return device // quarter, lax.rem(device, quarter), lax.axis_index("tensor")


def pair_kernel(x_ref, out_ref, got, send_sem, recv_sem):
    peer = (lax.axis_index("dp"), 1 - lax.axis_index("tensor"))
    greet([peer])
    copy = remote(x_ref, got, send_sem, recv_sem, peer)
    copy.start()
    copy.wait()
    out_ref[...] = x_ref[...].astype(jnp.float32) + got[...].astype(jnp.float32)


def pair_sum(x, number):
    return pl.pallas_call(
        pair_kernel,
        out_shape=jax.ShapeDtypeStruct(x.shape, jnp.float32),
        in_specs=in_vmem(1),
        out_specs=in_vmem(1)[0],
        scratch_shapes=[
            pltpu.VMEM(x.shape, x.dtype),
            pltpu.SemaphoreType.DMA,
            pltpu.SemaphoreType.DMA,
        ],
        compiler_params=params(number),
    )(x)


def all_peers(experts, quarter, e, q, t):
    lines = [(lax.rem(e + k, experts) * quarter + q, t) for k in range(1, experts)]
    planes = [(e * quarter + lax.rem(q + m, quarter), t) for m in range(1, quarter)]
    return [None] + lines, [None] + planes, (e * quarter + q, 1 - t)


def dispatch_kernel(experts, quarter, picked, out, s1, r1, s2, r2, s3, r3):
    e, q, t = place(quarter)
    lines, planes, partner = all_peers(experts, quarter, e, q, t)
    greet(lines[1:] + planes[1:] + [partner])
    sent = []
    hops = {}
    for k in range(1, experts):
        copy = remote(
            picked.at[t, lax.rem(e + k, experts)], out.at[t, q, e], s1.at[k], r1.at[k], lines[k]
        )
        copy.start()
        sent.append(copy)
        hops[k] = copy
    spread = {}
    shared = []
    for k in range(experts):
        came = lax.rem(e - k + experts, experts)
        if k == 0:
            block = picked.at[t, e]
            out[t, q, e] = picked[t, e]
        else:
            hops[k].wait_recv()
            block = out.at[t, q, came]
        for m in range(1, quarter):
            copy = remote(block, out.at[t, q, came], s2.at[m, k], r2.at[m, k], planes[m])
            copy.start()
            sent.append(copy)
            spread[m, k] = copy
        copy = remote(block, out.at[t, q, came], s3.at[0, k], r3.at[0, k], partner)
        copy.start()
        sent.append(copy)
        shared.append(copy)
    for k in range(experts):
        came = lax.rem(e - k + experts, experts)
        for m in range(1, quarter):
            side = lax.rem(q - m + quarter, quarter)
            spread[m, k].wait_recv()
            block = out.at[t, side, came]
            copy = remote(block, block, s3.at[m, k], r3.at[m, k], partner)
            copy.start()
            sent.append(copy)
            shared.append(copy)
    for copy in shared:
        copy.wait_recv()
    for copy in sent:
        copy.wait_send()


def dispatch(picked, quarter):
    _, experts, capacity, width = picked.shape
    sems = [(experts,), (experts,)] + [(quarter, experts)] * 4
    return pl.pallas_call(
        functools.partial(dispatch_kernel, experts, quarter),
        out_shape=jax.ShapeDtypeStruct((2, quarter, experts, capacity, width), picked.dtype),
        in_specs=in_vmem(1),
        out_specs=in_vmem(1)[0],
        scratch_shapes=[pltpu.SemaphoreType.DMA(shape) for shape in sems],
        compiler_params=params(2),
    )(picked)


def collect_kernel(
    experts, quarter, part, out, got0, sum0, got1, acc, low, s0, r0, s1, r1, s2, r2, s3, r3
):
    e, q, t = place(quarter)
    lines, planes, partner = all_peers(experts, quarter, e, q, t)
    greet(lines[1:] + planes[1:] + [partner])
    sent = []
    firsts = {}
    order = list(range(1, quarter)) + [0]
    for m in order:
        side = lax.rem(q + m, quarter)
        copy = remote(part.at[1 - t, side], got0.at[m], s0.at[m], r0.at[m], partner)
        copy.start()
        sent.append(copy)
        firsts[m] = copy
    seconds = {}
    for m in order:
        side = lax.rem(q + m, quarter)
        firsts[m].wait_recv()
        total = part[t, side].astype(jnp.float32) + got0[m].astype(jnp.float32)
        if m == 0:
            acc[...] = total
        else:
            sum0[m] = total.astype(jnp.bfloat16)
            copy = remote(sum0.at[m], got1.at[m], s1.at[m], r1.at[m], planes[m])
            copy.start()
            sent.append(copy)
            seconds[m] = copy
    for m in range(1, quarter):
        seconds[m].wait_recv()
    total = acc[...]
    for m in range(1, quarter):
        total = total + got1[m].astype(jnp.float32)
    low[...] = total.astype(jnp.bfloat16)
    thirds = {}
    for k in range(1, experts):
        copy = remote(
            low.at[lax.rem(e + k, experts)], out.at[t, e], s2.at[k], r2.at[k], lines[k]
        )
        copy.start()
        sent.append(copy)
        thirds[k] = copy
    out[t, e] = low[e]
    shared = []
    for k in range(experts):
        came = lax.rem(e - k + experts, experts)
        if k == 0:
            block = low.at[e]
        else:
            thirds[k].wait_recv()
            block = out.at[t, came]
        copy = remote(block, out.at[t, came], s3.at[k], r3.at[k], partner)
        copy.start()
        sent.append(copy)
        shared.append(copy)
    for copy in shared:
        copy.wait_recv()
    for copy in sent:
        copy.wait_send()


def collect(part):
    _, quarter, experts, capacity, width = part.shape
    low = part.dtype
    block = (experts, capacity, width)
    sems = [(quarter,)] * 4 + [(experts,)] * 4
    return pl.pallas_call(
        functools.partial(collect_kernel, experts, quarter),
        out_shape=jax.ShapeDtypeStruct((2, experts, capacity, width), low),
        in_specs=in_vmem(1),
        out_specs=in_vmem(1)[0],
        scratch_shapes=[
            pltpu.VMEM((quarter,) + block, low),
            pltpu.VMEM((quarter,) + block, low),
            pltpu.VMEM((quarter,) + block, low),
            pltpu.VMEM(block, jnp.float32),
            pltpu.VMEM(block, low),
        ]
        + [pltpu.SemaphoreType.DMA(shape) for shape in sems],
        compiler_params=params(3),
    )(part)


def reduce_kernel(
    experts, quarter, g, small, out, small_out,
    got1, sum1, got2, tiny1, mid, tiny2,
    s1, r1, s2, r2, s3, r3, s4, r4, s5, r5, s6, r6,
):
    e, q, t = place(quarter)
    lines, planes, _ = all_peers(experts, quarter, e, q, t)
    greet(lines[1:] + planes[1:])
    sent = []
    tiny = []
    for m in range(1, quarter):
        copy = remote(small, tiny1.at[q], s5.at[m], r5.at[m], planes[m])
        copy.start()
        sent.append(copy)
        tiny.append(copy)
    tiny1[q] = small[...]
    order = list(range(1, experts)) + [0]
    firsts = {}
    for k in order:
        for m in range(1, quarter):
            copy = remote(
                g.at[lax.rem(q + m, quarter), lax.rem(e + k, experts)],
                got1.at[m, k],
                s1.at[m, k],
                r1.at[m, k],
                planes[m],
            )
            copy.start()
            sent.append(copy)
            firsts[m, k] = copy
    for copy in tiny:
        copy.wait_recv()
    total = tiny1[0]
    for m in range(1, quarter):
        total = total + tiny1[m]
    mid[...] = total
    tiny2[e] = total
    tiny = []
    for k in range(1, experts):
        copy = remote(mid, tiny2.at[e], s6.at[k], r6.at[k], lines[k])
        copy.start()
        sent.append(copy)
        tiny.append(copy)
    seconds = {}
    for k in order:
        total = g[q, lax.rem(e + k, experts)].astype(jnp.float32)
        for m in range(1, quarter):
            firsts[m, k].wait_recv()
            total = total + got1[m, k].astype(jnp.float32)
        if k > 0:
            sum1[k] = total.astype(jnp.bfloat16)
            copy = remote(sum1.at[k], got2.at[k], s2.at[k], r2.at[k], lines[k])
            copy.start()
            sent.append(copy)
            seconds[k] = copy
    for k in range(1, experts):
        seconds[k].wait_recv()
        total = total + got2[k].astype(jnp.float32)
    sum1[0] = total.astype(jnp.bfloat16)
    out[q, e] = total.astype(jnp.bfloat16)
    thirds = {}
    for k in range(1, experts):
        copy = remote(sum1.at[0], out.at[q, e], s3.at[k], r3.at[k], lines[k])
        copy.start()
        sent.append(copy)
        thirds[k] = copy
    last = []
    for k in range(experts):
        came = lax.rem(e - k + experts, experts)
        if k == 0:
            block = sum1.at[0]
        else:
            thirds[k].wait_recv()
            block = out.at[q, came]
        for m in range(1, quarter):
            copy = remote(block, out.at[q, came], s4.at[m, k], r4.at[m, k], planes[m])
            copy.start()
            sent.append(copy)
            last.append(copy)
    for copy in tiny:
        copy.wait_recv()
    total = tiny2[0]
    for k in range(1, experts):
        total = total + tiny2[k]
    small_out[...] = total
    for copy in last:
        copy.wait_recv()
    for copy in sent:
        copy.wait_send()


def reduce_all(g, small):
    quarter, experts, piece, width = g.shape
    low = g.dtype
    both = (quarter, experts)
    sems = [both, both] + [(experts,)] * 4 + [both, both] + [(quarter,)] * 2 + [(experts,)] * 2
    return pl.pallas_call(
        functools.partial(reduce_kernel, experts, quarter),
        out_shape=(
            jax.ShapeDtypeStruct(g.shape, low),
            jax.ShapeDtypeStruct(small.shape, jnp.float32),
        ),
        in_specs=in_vmem(2),
        out_specs=tuple(in_vmem(2)),
        scratch_shapes=[
            pltpu.VMEM(g.shape, low),
            pltpu.VMEM((experts, piece, width), low),
            pltpu.VMEM((experts, piece, width), low),
            pltpu.VMEM((quarter,) + small.shape, jnp.float32),
            pltpu.VMEM(small.shape, jnp.float32),
            pltpu.VMEM((experts,) + small.shape, jnp.float32),
        ]
        + [pltpu.SemaphoreType.DMA(shape) for shape in sems],
        compiler_params=params(4),
    )(g, small)


def bias_kernel(rows, relative, out):
    span = relative.shape[1]
    for head in range(out.shape[0]):
        wide = jnp.broadcast_to(relative[head : head + 1, :], (rows, span))
        turned = pltpu.roll(wide, span - rows + 1, 1, stride=1, stride_axis=0)
        out[head] = turned[:, :rows]


def bias_of(relative, rows):
    heads = relative.shape[1]
    span = 2 * rows
    wide = jnp.pad(relative.T, ((0, 0), (0, span - relative.shape[0])))
    return pl.pallas_call(
        functools.partial(bias_kernel, rows),
        out_shape=jax.ShapeDtypeStruct((heads, rows, rows), jnp.float32),
        in_specs=in_vmem(1),
        out_specs=in_vmem(1)[0],
    )(wide)


def rows_up(amount, step):
    return (amount + step - 1) // step * step


def reduce_grads(large, small, experts, quarter):
    width = large[0].shape[1]
    stack = jnp.concatenate([one.astype(jnp.bfloat16) for one in large], axis=0)
    rows = stack.shape[0]
    piece = rows_up(-(-rows // (experts * quarter)), 16)
    stack = jnp.pad(stack, ((0, piece * experts * quarter - rows), (0, 0)))
    flat = jnp.concatenate([one.reshape(-1) for one in small])
    amount = flat.shape[0]
    flat = jnp.pad(flat, (0, rows_up(amount, 1024) - amount)).reshape(-1, 128)
    done, tiny = reduce_all(stack.reshape(quarter, experts, piece, width), flat)
    done = done.reshape(-1, width)
    tiny = tiny.reshape(-1)
    wide, at = [], 0
    for one in large:
        wide.append(done[at : at + one.shape[0]].astype(jnp.float32))
        at += one.shape[0]
    thin, at = [], 0
    for one in small:
        thin.append(tiny[at : at + one.size].reshape(one.shape))
        at += one.size
    return wide, thin


def scores_of(queries, keys, bias, allowed):
    raw = jnp.einsum("ihc,jhc->hij", queries, keys, preferred_element_type=jnp.float32) + bias
    return jnp.where(allowed[None], raw, -1e30)


def expert_forward(arrived, expert_in, expert_out):
    pre = jnp.dot(arrived, expert_in, preferred_element_type=jnp.float32)
    act_full, gelu_back = jax.vjp(jax.nn.gelu, pre)
    act = act_full.astype(jnp.bfloat16)
    part = jnp.dot(act, expert_out, preferred_element_type=jnp.float32)
    return (act, gelu_back, part)


def expert_backward(arrived_grad, gelu_back, expert_in, expert_out):
    act_grad = jnp.einsum("rd,fd->rf", arrived_grad, expert_out, preferred_element_type=jnp.float32)
    pre_grad = gelu_back(act_grad)[0].astype(jnp.bfloat16)
    input_part = jnp.einsum("rf,df->rd", pre_grad, expert_in, preferred_element_type=jnp.float32)
    return (pre_grad, input_part)


def local(
    tokens,
    cotangent,
    seq_lengths,
    seq_owner,
    routes,
    rel_buckets,
    attn_gain,
    query_weight,
    key_weight,
    value_weight,
    output_weight,
    bias_table,
    ffn_gain,
    router_weight,
    expert_in,
    expert_out,
):
    rows = tokens.shape[0]
    local_heads = query_weight.shape[1] // HEAD_DIM
    experts = router_weight.shape[1]
    groups = lax.axis_size("dp")
    quarter = groups // experts
    capacity = rows_up(max(2, 4 * rows // (3 * experts)), 16)
    segment, valid = block_layout(seq_lengths, seq_owner, rows)
    keep = valid.astype(jnp.float32)
    inputs = tokens.astype(jnp.float32)
    normed_full, scale_one = rms_rows(inputs, attn_gain)
    normed = normed_full.astype(jnp.bfloat16)
    queries = (
        jnp.dot(normed, query_weight, preferred_element_type=jnp.float32)
        .astype(jnp.bfloat16)
        .reshape(rows, local_heads, HEAD_DIM)
    )
    keys = (
        jnp.dot(normed, key_weight, preferred_element_type=jnp.float32)
        .astype(jnp.bfloat16)
        .reshape(rows, local_heads, HEAD_DIM)
    )
    values = (
        jnp.dot(normed, value_weight, preferred_element_type=jnp.float32)
        .astype(jnp.bfloat16)
        .reshape(rows, local_heads, HEAD_DIM)
    )
    positions = jnp.arange(rows, dtype=jnp.int32)
    lookup = (
        rel_buckets[:, None] == jnp.arange(bias_table.shape[0], dtype=jnp.int32)[None, :]
    ).astype(jnp.float32)
    relative = jnp.dot(lookup, bias_table, precision=lax.Precision.HIGHEST)
    bias = bias_of(relative, rows)
    allowed = (segment[:, None] == segment[None, :]) & valid[:, None] | (
        positions[:, None] == positions[None, :]
    )
    scores = scores_of(queries, keys, bias, allowed)
    top = jnp.max(scores, axis=-1, keepdims=True)
    weights = jnp.exp(scores - top)
    total = jnp.sum(weights, axis=-1, keepdims=True)
    probs = (weights / total).astype(jnp.bfloat16)
    log_total = top + jnp.log(total)
    mixed = (
        jnp.einsum("hij,jhc->ihc", probs, values, preferred_element_type=jnp.float32)
        .astype(jnp.bfloat16)
        .reshape(rows, -1)
    )
    attn_part = jnp.dot(mixed, output_weight, preferred_element_type=jnp.float32)
    attended = pair_sum(attn_part, 0) * keep[:, None]
    middle = inputs + attended
    normed_two_full, scale_two = rms_rows(middle, ffn_gain)
    normed_two = normed_two_full.astype(jnp.bfloat16)
    logits = jnp.dot(normed_two, router_weight, preferred_element_type=jnp.float32)
    gate_probs = jax.nn.softmax(logits, axis=-1)
    chosen = routes[:, 0]
    expert_ids = jnp.arange(experts, dtype=jnp.int32)
    route_hot = chosen[:, None] == expert_ids[None, :]
    gate = jnp.sum(gate_probs * route_hot.astype(jnp.float32), axis=-1)
    picked = (route_hot & valid[:, None]).astype(jnp.int32)
    before = (positions[None, :] < positions[:, None]).astype(jnp.bfloat16)
    ahead = jnp.dot(before, picked.astype(jnp.bfloat16), preferred_element_type=jnp.float32)
    rank = jnp.sum(ahead.astype(jnp.int32) * picked, axis=1)
    slot = jnp.where(valid, chosen * capacity + rank, experts * capacity)
    places = jnp.arange(experts * capacity, dtype=jnp.int32)
    match = slot[None, :] == places[:, None]
    chooser = match.astype(jnp.bfloat16)
    grad_out = cotangent.astype(jnp.float32)
    expert_grad = (gate[:, None] * grad_out).astype(jnp.bfloat16)
    width = tokens.shape[1]
    chosen_rows = jnp.dot(
        chooser,
        jnp.concatenate([normed_two, expert_grad], axis=1),
        preferred_element_type=jnp.float32,
    ).astype(jnp.bfloat16)
    shipped = jnp.stack([chosen_rows[:, :width], chosen_rows[:, width:]])
    landed = dispatch(shipped.reshape(2, experts, capacity, width), quarter)
    landed = landed.reshape(2, groups * capacity, width)
    arrived, arrived_grad = landed[0], landed[1]
    act, gelu_back, part = expert_forward(arrived, expert_in, expert_out)
    pre_grad, input_part = expert_backward(arrived_grad, gelu_back, expert_in, expert_out)
    partial = jnp.stack([part.astype(jnp.bfloat16), input_part.astype(jnp.bfloat16)])
    returned = collect(partial.reshape(2, quarter, experts, capacity, width))
    returned = returned.reshape(2, experts * capacity, width)
    back = jnp.einsum(
        "pt,apd->atd", chooser, returned, preferred_element_type=jnp.float32
    )
    expert_rows, expert_input_grad = back[0], back[1]
    output = (middle + gate[:, None] * expert_rows).astype(jnp.bfloat16)
    gate_grad = jnp.sum(grad_out * expert_rows, axis=-1)
    logit_grad = (
        gate_probs * (route_hot.astype(jnp.float32) - gate[:, None]) * gate_grad[:, None]
    ).astype(jnp.bfloat16)
    router_grad = jnp.einsum(
        "td,te->de", normed_two, logit_grad, preferred_element_type=jnp.float32
    )
    expert_out_grad = jnp.einsum("rf,rd->fd", act, arrived_grad, preferred_element_type=jnp.float32)
    expert_in_grad = jnp.einsum("rd,rf->df", arrived, pre_grad, preferred_element_type=jnp.float32)
    normed_two_grad = expert_input_grad + jnp.einsum(
        "te,de->td", logit_grad, router_weight, preferred_element_type=jnp.float32
    )
    middle_part, ffn_gain_grad = rms_back(middle, ffn_gain, scale_two, normed_two_grad)
    middle_grad = grad_out + middle_part
    attn_grad = (middle_grad * keep[:, None]).astype(jnp.bfloat16)
    output_weight_grad = jnp.einsum(
        "tc,td->cd", mixed, attn_grad, preferred_element_type=jnp.float32
    )
    mixed_grad = (
        jnp.einsum("td,cd->tc", attn_grad, output_weight, preferred_element_type=jnp.float32)
        .astype(jnp.bfloat16)
        .reshape(rows, local_heads, HEAD_DIM)
    )
    scores_again = scores_of(queries, keys, bias, allowed)
    probs_full = jnp.exp(scores_again - log_total)
    probs_low = probs_full.astype(jnp.bfloat16)
    prob_grad = jnp.einsum("ihc,jhc->hij", mixed_grad, values, preferred_element_type=jnp.float32)
    values_grad = jnp.einsum(
        "hij,ihc->jhc", probs_low, mixed_grad, preferred_element_type=jnp.float32
    ).astype(jnp.bfloat16)
    score_grad = (
        probs_full * (prob_grad - jnp.sum(probs_full * prob_grad, axis=-1, keepdims=True))
    ).astype(jnp.bfloat16)
    queries_grad = (
        jnp.einsum("hij,jhc->ihc", score_grad, keys, preferred_element_type=jnp.float32)
        .astype(jnp.bfloat16)
        .reshape(rows, -1)
    )
    keys_grad = (
        jnp.einsum("hij,ihc->jhc", score_grad, queries, preferred_element_type=jnp.float32)
        .astype(jnp.bfloat16)
        .reshape(rows, -1)
    )
    values_grad = values_grad.reshape(rows, -1)
    table_grad = jnp.dot(
        lookup.T, diagonal_sums(score_grad.astype(jnp.float32)).T, precision=lax.Precision.HIGHEST
    )
    query_grad = jnp.einsum("td,tc->dc", normed, queries_grad, preferred_element_type=jnp.float32)
    key_grad = jnp.einsum("td,tc->dc", normed, keys_grad, preferred_element_type=jnp.float32)
    value_grad = jnp.einsum("td,tc->dc", normed, values_grad, preferred_element_type=jnp.float32)
    normed_part = (
        jnp.einsum("tc,dc->td", queries_grad, query_weight, preferred_element_type=jnp.float32)
        + jnp.einsum("tc,dc->td", keys_grad, key_weight, preferred_element_type=jnp.float32)
        + jnp.einsum("tc,dc->td", values_grad, value_weight, preferred_element_type=jnp.float32)
    )
    normed_grad = pair_sum(normed_part.astype(jnp.bfloat16), 1)
    input_part_grad, attn_gain_grad = rms_back(inputs, attn_gain, scale_one, normed_grad)
    tokens_grad = (middle_grad + input_part_grad).astype(jnp.bfloat16)
    half = output_weight_grad.shape[0]
    pieces = [output_weight_grad[:, at : at + half] for at in range(0, width, half)]
    wide, thin = reduce_grads(
        [query_grad, key_grad, value_grad] + pieces,
        [attn_gain_grad, table_grad, ffn_gain_grad, router_grad],
        experts,
        quarter,
    )
    summed = (
        thin[0],
        wide[0],
        wide[1],
        wide[2],
        jnp.concatenate(wide[3:], axis=1),
        thin[1],
        thin[2],
        thin[3],
    )
    return (
        output,
        tokens_grad,
        summed[0],
        summed[1],
        summed[2],
        summed[3],
        summed[4],
        summed[5],
        summed[6],
        summed[7],
        expert_in_grad,
        expert_out_grad,
    )


def solution(mesh):
    return jax.shard_map(
        local,
        mesh=mesh,
        in_specs=(
            P("dp", None),
            P("dp", None),
            P(),
            P(),
            P("dp", None),
            P(),
            P(),
            P(None, "tensor"),
            P(None, "tensor"),
            P(None, "tensor"),
            P("tensor", None),
            P(None, "tensor"),
            P(),
            P(),
            P(None, ("dp", "tensor")),
            P(("dp", "tensor"), None),
        ),
        out_specs=(
            P("dp", None),
            P("dp", None),
            P(),
            P(None, "tensor"),
            P(None, "tensor"),
            P(None, "tensor"),
            P("tensor", None),
            P(None, "tensor"),
            P(),
            P(),
            P(None, ("dp", "tensor")),
            P(("dp", "tensor"), None),
        ),
        check_vma=False,
    )
```

```python
import functools

import jax
import jax.numpy as jnp
from jax import lax
from jax.experimental import pallas as pl
from jax.experimental.pallas import tpu as pltpu
from jax.sharding import PartitionSpec as P

HEAD_DIM = 64


epsilon = 1e-06


def rms_rows(rows, gain):
    scale = lax.rsqrt(jnp.mean(rows * rows, axis=-1, keepdims=True) + epsilon)
    return (rows * scale * gain, scale)


def rms_back(rows, gain, scale, grad):
    gain_grad = jnp.sum(grad * rows * scale, axis=0)
    inner = jnp.mean(rows * gain * grad, axis=-1, keepdims=True)
    return (scale * (gain * grad) - rows * (scale * scale * scale) * inner, gain_grad)


def block_layout(seq_lengths, seq_owner, rows):
    device = lax.axis_index("dp")
    mine = (seq_owner == device).astype(jnp.int32)
    owned = mine * seq_lengths
    order = jnp.arange(owned.shape[0], dtype=jnp.int32)
    starts = jnp.sum(jnp.where(order[None, :] < order[:, None], owned[None, :], 0), axis=1)
    slots = jnp.arange(rows, dtype=jnp.int32)
    inside = (
        (mine[:, None] > 0)
        & (slots[None, :] >= starts[:, None])
        & (slots[None, :] < (starts + owned)[:, None])
    ).astype(jnp.int32)
    count = jnp.sum(inside, axis=0)
    numbers = jnp.arange(seq_lengths.shape[0], dtype=jnp.int32)
    segment = jnp.sum(inside * numbers[:, None], axis=0)
    return (jnp.where(count > 0, segment, -1), count > 0)


def diagonal_sums(square):
    heads = square.shape[0]
    length = square.shape[1]
    flipped = square[:, ::-1, :]
    padded = jnp.pad(flipped, ((0, 0), (0, 0), (0, length)))
    flat = padded.reshape(heads, 2 * length * length)[:, : length * (2 * length - 1)]
    return jnp.sum(flat.reshape(heads, length, 2 * length - 1), axis=1)


MESH = pl.DeviceIdType.MESH
LIMIT = 48 * 1024 * 1024


def params(number):
    return pltpu.CompilerParams(
        collective_id=number, has_side_effects=True, vmem_limit_bytes=LIMIT
    )


def in_vmem(count):
    return [pl.BlockSpec(memory_space=pltpu.VMEM)] * count


def greet(peers):
    barrier = pltpu.get_barrier_semaphore()
    for peer in peers:
        pl.semaphore_signal(barrier, inc=1, device_id=peer, device_id_type=MESH)
    pl.semaphore_wait(barrier, len(peers))


def remote(src, dst, send_sem, recv_sem, peer):
    return pltpu.make_async_remote_copy(
        src_ref=src,
        dst_ref=dst,
        send_sem=send_sem,
        recv_sem=recv_sem,
        device_id=peer,
        device_id_type=MESH,
    )


def place(quarter):
    device = lax.axis_index("dp")
    return device // quarter, lax.rem(device, quarter), lax.axis_index("tensor")


def pair_kernel(x_ref, out_ref, got, send_sem, recv_sem):
    peer = (lax.axis_index("dp"), 1 - lax.axis_index("tensor"))
    greet([peer])
    copy = remote(x_ref, got, send_sem, recv_sem, peer)
    copy.start()
    copy.wait()
    out_ref[...] = x_ref[...].astype(jnp.float32) + got[...].astype(jnp.float32)


def pair_sum(x, number):
    return pl.pallas_call(
        pair_kernel,
        out_shape=jax.ShapeDtypeStruct(x.shape, jnp.float32),
        in_specs=in_vmem(1),
        out_specs=in_vmem(1)[0],
        scratch_shapes=[
            pltpu.VMEM(x.shape, x.dtype),
            pltpu.SemaphoreType.DMA,
            pltpu.SemaphoreType.DMA,
        ],
        compiler_params=params(number),
    )(x)


def line_peers(experts, quarter, e, q, t):
    return [None] + [(lax.rem(e + k, experts) * quarter + q, t) for k in range(1, experts)]


def plane_of(quarter, e, q, t):
    y, x = q // 2, lax.rem(q, 2)
    beside = 2 * y + (1 - x)
    below = 2 * (1 - y) + x
    across = 2 * (1 - y) + (1 - x)
    return (beside, below, across), (e * quarter + beside, t), (e * quarter + below, t)


def part_of(ref, index, side):
    half = ref.shape[-1] // 2
    return ref.at[index + (slice(None), pl.ds(side * half, half))]


def scatter_plane(g, ready, done, experts, e, q, sides, near, got, relay, got2, s1, r1, s2, r2):
    beside, below, across = sides
    first = near
    second = (near[1], near[0])
    keeps = (beside, below)
    passes = (below, beside)
    order = list(range(1, experts)) + [0]
    sent = []
    firsts = {}
    seconds = {}
    for k in order:
        ed = lax.rem(e + k, experts)
        ready(k, ed)
        for j, piece_of in ((0, lambda i: across), (1, lambda i: keeps[i])):
            for i in range(2):
                copy = remote(
                    part_of(g, (piece_of(i), ed), i),
                    got.at[i, k, j],
                    s1.at[i, k, j],
                    r1.at[i, k, j],
                    first[i],
                )
                copy.start()
                sent.append(copy)
                firsts[i, k, j] = copy

    def finish(k):
        ed = lax.rem(e + k, experts)
        totals = []
        for i in range(2):
            firsts[i, k, 1].wait_recv()
            seconds[i, k].wait_recv()
            totals.append(
                part_of(g, (q, ed), i)[...].astype(jnp.float32)
                + got[i, k, 1].astype(jnp.float32)
                + got2[i, k].astype(jnp.float32)
            )
        done(k, ed, totals)

    for at, k in enumerate(order):
        ed = lax.rem(e + k, experts)
        for i in range(2):
            firsts[i, k, 0].wait_recv()
            relay[i, k] = (
                part_of(g, (passes[i], ed), i)[...].astype(jnp.float32)
                + got[i, k, 0].astype(jnp.float32)
            ).astype(jnp.bfloat16)
            copy = remote(relay.at[i, k], got2.at[i, k], s2.at[i, k], r2.at[i, k], second[i])
            copy.start()
            sent.append(copy)
            seconds[i, k] = copy
        if at > 0:
            finish(order[at - 1])
    finish(order[-1])
    return sent


def plane_scratch(experts, block, low):
    half = (block[0], block[1] // 2)
    return [
        pltpu.VMEM((2, experts, 2) + half, low),
        pltpu.VMEM((2, experts) + half, low),
        pltpu.VMEM((2, experts) + half, low),
        pltpu.SemaphoreType.DMA((2, experts, 2)),
        pltpu.SemaphoreType.DMA((2, experts, 2)),
        pltpu.SemaphoreType.DMA((2, experts)),
        pltpu.SemaphoreType.DMA((2, experts)),
    ]


def gather_plane(out, lead, blocks, experts, e, q, sides, near, arrived, s1, r1, s2, r2):
    beside, below, across = sides
    sent = []
    firsts = {}
    for k in range(experts):
        came = lax.rem(e - k + experts, experts)
        block = blocks(k, came)
        for i in range(2):
            copy = remote(block, out.at[lead + (q, came)], s1.at[i, k], r1.at[i, k], near[i])
            copy.start()
            sent.append(copy)
            firsts[i, k] = copy
    seconds = {}
    for k in range(experts):
        came = lax.rem(e - k + experts, experts)
        for i in range(2):
            firsts[i, k].wait_recv()
            ref = part_of(out, lead + ((beside, below)[i], came), i)
            copy = remote(ref, ref, s2.at[i, k], r2.at[i, k], near[1 - i])
            copy.start()
            sent.append(copy)
            seconds[i, k] = copy
            arrived(out.at[lead + ((beside, below)[i], came)], i, k)
    for k in range(experts):
        came = lax.rem(e - k + experts, experts)
        for i in range(2):
            seconds[i, k].wait_recv()
        arrived(out.at[lead + (across, came)], 2, k)
    return sent


def dispatch_kernel(experts, quarter, picked, out, s1, r1, s2, r2, s3, r3, s4, r4):
    e, q, t = place(quarter)
    lines = line_peers(experts, quarter, e, q, t)
    sides, beside, below = plane_of(quarter, e, q, t)
    partner = (e * quarter + q, 1 - t)
    greet(lines[1:] + [beside, below, partner])
    sent = []
    hops = {}
    for k in range(1, experts):
        copy = remote(
            picked.at[t, lax.rem(e + k, experts)], out.at[t, q, e], s1.at[k], r1.at[k], lines[k]
        )
        copy.start()
        sent.append(copy)
        hops[k] = copy
    out[t, q, e] = picked[t, e]
    shared = []

    def share(src, dst, i, k):
        copy = remote(src, dst, s4.at[i, k], r4.at[i, k], partner)
        copy.start()
        sent.append(copy)
        shared.append(copy)

    def block(k, came):
        if k == 0:
            src = picked.at[t, e]
        else:
            hops[k].wait_recv()
            src = out.at[t, q, came]
        share(src, out.at[t, q, came], 3, k)
        return src

    sent += gather_plane(
        out, (t,), block, experts, e, q, sides, (beside, below),
        lambda ref, i, k: share(ref, ref, i, k), s2, r2, s3, r3,
    )
    for copy in shared:
        copy.wait_recv()
    for copy in sent:
        copy.wait_send()


def dispatch(picked, quarter):
    assert quarter == 4
    _, experts, capacity, width = picked.shape
    sems = [(experts,)] * 2 + [(2, experts)] * 4 + [(4, experts)] * 2
    return pl.pallas_call(
        functools.partial(dispatch_kernel, experts, quarter),
        out_shape=jax.ShapeDtypeStruct((2, quarter, experts, capacity, width), picked.dtype),
        in_specs=in_vmem(1),
        out_specs=in_vmem(1)[0],
        scratch_shapes=[pltpu.SemaphoreType.DMA(shape) for shape in sems],
        compiler_params=params(2),
    )(picked)


def collect_kernel(
    experts, quarter, part, out, got0, sum0, low, s0, r0, s3, r3, s4, r4,
    got, relay, got2, s1, r1, s2, r2,
):
    e, q, t = place(quarter)
    lines = line_peers(experts, quarter, e, q, t)
    sides, beside, below = plane_of(quarter, e, q, t)
    partner = (e * quarter + q, 1 - t)
    greet(lines[1:] + [beside, below, partner])
    sent = []
    halves = {}
    places = (sides[2], sides[0], sides[1], q)
    for k in list(range(1, experts)) + [0]:
        ed = lax.rem(e + k, experts)
        for m in range(quarter):
            copy = remote(
                part.at[1 - t, places[m], ed],
                got0.at[places[m], ed],
                s0.at[m, k],
                r0.at[m, k],
                partner,
            )
            copy.start()
            sent.append(copy)
            halves[m, k] = copy

    def ready(k, ed):
        for m in range(quarter):
            halves[m, k].wait_recv()
            sum0[places[m], ed] = (
                part[t, places[m], ed].astype(jnp.float32)
                + got0[places[m], ed].astype(jnp.float32)
            ).astype(jnp.bfloat16)

    thirds = {}
    width = low.shape[-1]

    def done(k, ed, totals):
        for i in range(2):
            low[k, :, i * width // 2 : (i + 1) * width // 2] = totals[i].astype(jnp.bfloat16)
        if k > 0:
            copy = remote(low.at[k], out.at[t, e], s3.at[k], r3.at[k], lines[k])
            copy.start()
            sent.append(copy)
            thirds[k] = copy

    sent += scatter_plane(
        sum0, ready, done, experts, e, q, sides, (beside, below),
        got, relay, got2, s1, r1, s2, r2,
    )
    out[t, e] = low[0]
    shared = []
    for k in range(experts):
        came = lax.rem(e - k + experts, experts)
        if k == 0:
            block = low.at[0]
        else:
            thirds[k].wait_recv()
            block = out.at[t, came]
        copy = remote(block, out.at[t, came], s4.at[k], r4.at[k], partner)
        copy.start()
        sent.append(copy)
        shared.append(copy)
    for copy in shared:
        copy.wait_recv()
    for copy in sent:
        copy.wait_send()


def collect(part):
    _, quarter, experts, capacity, width = part.shape
    assert quarter == 4
    low = part.dtype
    block = (capacity, width)
    sems = [(quarter, experts)] * 2 + [(experts,)] * 4
    return pl.pallas_call(
        functools.partial(collect_kernel, experts, quarter),
        out_shape=jax.ShapeDtypeStruct((2, experts) + block, low),
        in_specs=in_vmem(1),
        out_specs=in_vmem(1)[0],
        scratch_shapes=[
            pltpu.VMEM((quarter, experts) + block, low),
            pltpu.VMEM((quarter, experts) + block, low),
            pltpu.VMEM((experts,) + block, low),
        ]
        + [pltpu.SemaphoreType.DMA(shape) for shape in sems]
        + plane_scratch(experts, block, low),
        compiler_params=params(3),
    )(part)


def reduce_kernel(
    experts, quarter, g, small, query_out, key_out, value_out, weight_out, small_out,
    out, sum1, got3, tiny1, mid, tiny2,
    s3, r3, s4, r4, s5, r5, s6, r6, s7, r7, s8, r8,
    got, relay, got2, s1, r1, s2, r2,
):
    e, q, t = place(quarter)
    lines = line_peers(experts, quarter, e, q, t)
    sides, beside, below = plane_of(quarter, e, q, t)
    across = (e * quarter + sides[2], t)
    planes = (beside, below, across)
    greet(lines[1:] + [beside, below, across])
    sent = []
    tiny = []
    for m in range(3):
        copy = remote(small, tiny1.at[q], s5.at[m], r5.at[m], planes[m])
        copy.start()
        sent.append(copy)
        tiny.append(copy)
    tiny1[q] = small[...]
    width = out.shape[-1]
    cols = [slice(i * width // 2, (i + 1) * width // 2) for i in range(2)]
    seconds = {}
    kept = []

    def done(k, ed, totals):
        if k > 0:
            for i in range(2):
                sum1[k, :, cols[i]] = totals[i].astype(jnp.bfloat16)
            copy = remote(sum1.at[k], got3.at[k], s3.at[k], r3.at[k], lines[k])
            copy.start()
            sent.append(copy)
            seconds[k] = copy
        else:
            kept.extend(totals)

    sent += scatter_plane(
        g, lambda k, ed: None, done, experts, e, q, sides, (beside, below),
        got, relay, got2, s1, r1, s2, r2,
    )
    for copy in tiny:
        copy.wait_recv()
    total = tiny1[0]
    for m in range(1, quarter):
        total = total + tiny1[m]
    mid[...] = total
    tiny2[e] = total
    tiny = []
    for k in range(1, experts):
        copy = remote(mid, tiny2.at[e], s6.at[k], r6.at[k], lines[k])
        copy.start()
        sent.append(copy)
        tiny.append(copy)
    for k in range(1, experts):
        seconds[k].wait_recv()
        for i in range(2):
            kept[i] = kept[i] + got3[k, :, cols[i]].astype(jnp.float32)
    for i in range(2):
        sum1[0, :, cols[i]] = kept[i].astype(jnp.bfloat16)
    out[q, e] = sum1[0]
    thirds = {}
    for k in range(1, experts):
        copy = remote(sum1.at[0], out.at[q, e], s4.at[k], r4.at[k], lines[k])
        copy.start()
        sent.append(copy)
        thirds[k] = copy

    def block(k, came):
        if k == 0:
            return sum1.at[0]
        thirds[k].wait_recv()
        return out.at[q, came]

    sent += gather_plane(
        out, (), block, experts, e, q, sides, (beside, below),
        lambda ref, i, k: None, s7, r7, s8, r8,
    )
    for copy in tiny:
        copy.wait_recv()
    total = tiny2[0]
    for k in range(1, experts):
        total = total + tiny2[k]
    small_out[...] = total
    for copy in sent:
        copy.wait_send()
    piece = out.shape[2]
    rows, half = query_out.shape
    for number in range(quarter * experts):
        at = number * piece
        if at < rows:
            whole = out[number // experts, number % experts].astype(jnp.float32)
            query_out[at : at + piece] = whole[:, :half]
            key_out[at : at + piece] = whole[:, half:]
        elif at < rows + half:
            at = at - rows
            whole = out[number // experts, number % experts].astype(jnp.float32)
            value_out[at : at + piece] = whole[:, :half]
            value_out[half + at : half + at + piece] = whole[:, half:]
        elif at < rows + 2 * half:
            at = at - rows - half
            whole = out[number // experts, number % experts].astype(jnp.float32)
            weight_out[at : at + piece] = whole


def reduce_all(g, small, rows, half):
    quarter, experts, piece, width = g.shape
    assert quarter == 4 and width == 2 * half and rows == 2 * half and half % piece == 0
    low = g.dtype
    sems = [(experts,)] * 4 + [(3,)] * 2 + [(experts,)] * 2 + [(2, experts)] * 4
    tall = jax.ShapeDtypeStruct((rows, half), jnp.float32)
    return pl.pallas_call(
        functools.partial(reduce_kernel, experts, quarter),
        out_shape=(
            tall,
            tall,
            tall,
            jax.ShapeDtypeStruct((half, width), jnp.float32),
            jax.ShapeDtypeStruct(small.shape, jnp.float32),
        ),
        in_specs=in_vmem(2),
        out_specs=tuple(in_vmem(5)),
        scratch_shapes=[
            pltpu.VMEM(g.shape, low),
            pltpu.VMEM((experts, piece, width), low),
            pltpu.VMEM((experts, piece, width), low),
            pltpu.VMEM((quarter,) + small.shape, jnp.float32),
            pltpu.VMEM(small.shape, jnp.float32),
            pltpu.VMEM((experts,) + small.shape, jnp.float32),
        ]
        + [pltpu.SemaphoreType.DMA(shape) for shape in sems]
        + plane_scratch(experts, (piece, width), low),
        compiler_params=params(4),
    )(g, small)


def bias_kernel(rows, relative, out):
    span = relative.shape[1]
    for head in range(out.shape[0]):
        wide = jnp.broadcast_to(relative[head : head + 1, :], (rows, span))
        turned = pltpu.roll(wide, span - rows + 1, 1, stride=1, stride_axis=0)
        out[head] = turned[:, :rows]


def bias_of(relative, rows):
    heads = relative.shape[1]
    span = 2 * rows
    wide = jnp.pad(relative.T, ((0, 0), (0, span - relative.shape[0])))
    return pl.pallas_call(
        functools.partial(bias_kernel, rows),
        out_shape=jax.ShapeDtypeStruct((heads, rows, rows), jnp.float32),
        in_specs=in_vmem(1),
        out_specs=in_vmem(1)[0],
    )(wide)


def rows_up(amount, step):
    return (amount + step - 1) // step * step


def reduce_grads(query, key, value, weight, small, experts, quarter):
    rows, half = query.shape
    query, key, value, weight = [
        one.astype(jnp.bfloat16) for one in (query, key, value, weight)
    ]
    stack = jnp.concatenate(
        [
            jnp.concatenate([query, key], axis=1),
            jnp.concatenate([value[:half], value[half:]], axis=1),
            weight,
        ],
        axis=0,
    )
    used, width = stack.shape
    piece = rows_up(-(-used // (experts * quarter)), 16)
    stack = jnp.pad(stack, ((0, piece * experts * quarter - used), (0, 0)))
    flat = jnp.concatenate([one.reshape(-1) for one in small])
    amount = flat.shape[0]
    flat = jnp.pad(flat, (0, rows_up(amount, 1024) - amount)).reshape(-1, 128)
    *wide, tiny = reduce_all(stack.reshape(quarter, experts, piece, width), flat, rows, half)
    tiny = tiny.reshape(-1)
    thin, at = [], 0
    for one in small:
        thin.append(tiny[at : at + one.size].reshape(one.shape))
        at += one.size
    return wide, thin


def scores_of(queries, keys, bias, allowed):
    raw = jnp.einsum("ihc,jhc->hij", queries, keys, preferred_element_type=jnp.float32) + bias
    return jnp.where(allowed[None], raw, -1e30)


def expert_forward(arrived, expert_in, expert_out):
    pre = jnp.dot(arrived, expert_in, preferred_element_type=jnp.float32)
    act_full, gelu_back = jax.vjp(jax.nn.gelu, pre)
    act = act_full.astype(jnp.bfloat16)
    part = jnp.dot(act, expert_out, preferred_element_type=jnp.float32)
    return (act, gelu_back, part)


def expert_backward(arrived_grad, gelu_back, expert_in, expert_out):
    act_grad = jnp.einsum("rd,fd->rf", arrived_grad, expert_out, preferred_element_type=jnp.float32)
    pre_grad = gelu_back(act_grad)[0].astype(jnp.bfloat16)
    input_part = jnp.einsum("rf,df->rd", pre_grad, expert_in, preferred_element_type=jnp.float32)
    return (pre_grad, input_part)


def local(
    tokens,
    cotangent,
    seq_lengths,
    seq_owner,
    routes,
    rel_buckets,
    attn_gain,
    query_weight,
    key_weight,
    value_weight,
    output_weight,
    bias_table,
    ffn_gain,
    router_weight,
    expert_in,
    expert_out,
):
    rows = tokens.shape[0]
    local_heads = query_weight.shape[1] // HEAD_DIM
    experts = router_weight.shape[1]
    groups = lax.axis_size("dp")
    quarter = groups // experts
    capacity = rows_up(max(2, 4 * rows // (3 * experts)), 16)
    segment, valid = block_layout(seq_lengths, seq_owner, rows)
    keep = valid.astype(jnp.float32)
    inputs = tokens.astype(jnp.float32)
    normed_full, scale_one = rms_rows(inputs, attn_gain)
    normed = normed_full.astype(jnp.bfloat16)
    queries = (
        jnp.dot(normed, query_weight, preferred_element_type=jnp.float32)
        .astype(jnp.bfloat16)
        .reshape(rows, local_heads, HEAD_DIM)
    )
    keys = (
        jnp.dot(normed, key_weight, preferred_element_type=jnp.float32)
        .astype(jnp.bfloat16)
        .reshape(rows, local_heads, HEAD_DIM)
    )
    values = (
        jnp.dot(normed, value_weight, preferred_element_type=jnp.float32)
        .astype(jnp.bfloat16)
        .reshape(rows, local_heads, HEAD_DIM)
    )
    positions = jnp.arange(rows, dtype=jnp.int32)
    lookup = (
        rel_buckets[:, None] == jnp.arange(bias_table.shape[0], dtype=jnp.int32)[None, :]
    ).astype(jnp.float32)
    relative = jnp.dot(lookup, bias_table, precision=lax.Precision.HIGHEST)
    bias = bias_of(relative, rows)
    allowed = (segment[:, None] == segment[None, :]) & valid[:, None] | (
        positions[:, None] == positions[None, :]
    )
    scores = scores_of(queries, keys, bias, allowed)
    top = jnp.max(scores, axis=-1, keepdims=True)
    weights = jnp.exp(scores - top)
    total = jnp.sum(weights, axis=-1, keepdims=True)
    probs = (weights / total).astype(jnp.bfloat16)
    log_total = top + jnp.log(total)
    mixed = (
        jnp.einsum("hij,jhc->ihc", probs, values, preferred_element_type=jnp.float32)
        .astype(jnp.bfloat16)
        .reshape(rows, -1)
    )
    attn_part = jnp.dot(mixed, output_weight, preferred_element_type=jnp.float32)
    attended = pair_sum(attn_part, 0) * keep[:, None]
    middle = inputs + attended
    normed_two_full, scale_two = rms_rows(middle, ffn_gain)
    normed_two = normed_two_full.astype(jnp.bfloat16)
    logits = jnp.dot(normed_two, router_weight, preferred_element_type=jnp.float32)
    gate_probs = jax.nn.softmax(logits, axis=-1)
    chosen = routes[:, 0]
    expert_ids = jnp.arange(experts, dtype=jnp.int32)
    route_hot = chosen[:, None] == expert_ids[None, :]
    gate = jnp.sum(gate_probs * route_hot.astype(jnp.float32), axis=-1)
    picked = (route_hot & valid[:, None]).astype(jnp.int32)
    before = (positions[None, :] < positions[:, None]).astype(jnp.bfloat16)
    ahead = jnp.dot(before, picked.astype(jnp.bfloat16), preferred_element_type=jnp.float32)
    rank = jnp.sum(ahead.astype(jnp.int32) * picked, axis=1)
    slot = jnp.where(valid, chosen * capacity + rank, experts * capacity)
    places = jnp.arange(experts * capacity, dtype=jnp.int32)
    match = slot[None, :] == places[:, None]
    chooser = match.astype(jnp.bfloat16)
    grad_out = cotangent.astype(jnp.float32)
    expert_grad = (gate[:, None] * grad_out).astype(jnp.bfloat16)
    width = tokens.shape[1]
    chosen_rows = jnp.dot(
        chooser,
        jnp.concatenate([normed_two, expert_grad], axis=1),
        preferred_element_type=jnp.float32,
    ).astype(jnp.bfloat16)
    shipped = jnp.stack([chosen_rows[:, :width], chosen_rows[:, width:]])
    landed = dispatch(shipped.reshape(2, experts, capacity, width), quarter)
    landed = landed.reshape(2, groups * capacity, width)
    arrived, arrived_grad = landed[0], landed[1]
    act, gelu_back, part = expert_forward(arrived, expert_in, expert_out)
    pre_grad, input_part = expert_backward(arrived_grad, gelu_back, expert_in, expert_out)
    partial = jnp.stack([part.astype(jnp.bfloat16), input_part.astype(jnp.bfloat16)])
    returned = collect(partial.reshape(2, quarter, experts, capacity, width))
    returned = returned.reshape(2, experts * capacity, width)
    back = jnp.einsum(
        "pt,apd->atd", chooser, returned, preferred_element_type=jnp.float32
    )
    expert_rows, expert_input_grad = back[0], back[1]
    output = (middle + gate[:, None] * expert_rows).astype(jnp.bfloat16)
    gate_grad = jnp.sum(grad_out * expert_rows, axis=-1)
    logit_grad = (
        gate_probs * (route_hot.astype(jnp.float32) - gate[:, None]) * gate_grad[:, None]
    ).astype(jnp.bfloat16)
    router_grad = jnp.einsum(
        "td,te->de", normed_two, logit_grad, preferred_element_type=jnp.float32
    )
    expert_out_grad = jnp.einsum("rf,rd->fd", act, arrived_grad, preferred_element_type=jnp.float32)
    expert_in_grad = jnp.einsum("rd,rf->df", arrived, pre_grad, preferred_element_type=jnp.float32)
    normed_two_grad = expert_input_grad + jnp.einsum(
        "te,de->td", logit_grad, router_weight, preferred_element_type=jnp.float32
    )
    middle_part, ffn_gain_grad = rms_back(middle, ffn_gain, scale_two, normed_two_grad)
    middle_grad = grad_out + middle_part
    attn_grad = (middle_grad * keep[:, None]).astype(jnp.bfloat16)
    output_weight_grad = jnp.einsum(
        "tc,td->cd", mixed, attn_grad, preferred_element_type=jnp.float32
    )
    mixed_grad = (
        jnp.einsum("td,cd->tc", attn_grad, output_weight, preferred_element_type=jnp.float32)
        .astype(jnp.bfloat16)
        .reshape(rows, local_heads, HEAD_DIM)
    )
    scores_again = scores_of(queries, keys, bias, allowed)
    probs_full = jnp.exp(scores_again - log_total)
    probs_low = probs_full.astype(jnp.bfloat16)
    prob_grad = jnp.einsum("ihc,jhc->hij", mixed_grad, values, preferred_element_type=jnp.float32)
    values_grad = jnp.einsum(
        "hij,ihc->jhc", probs_low, mixed_grad, preferred_element_type=jnp.float32
    ).astype(jnp.bfloat16)
    score_grad = (
        probs_full * (prob_grad - jnp.sum(probs_full * prob_grad, axis=-1, keepdims=True))
    ).astype(jnp.bfloat16)
    queries_grad = (
        jnp.einsum("hij,jhc->ihc", score_grad, keys, preferred_element_type=jnp.float32)
        .astype(jnp.bfloat16)
        .reshape(rows, -1)
    )
    keys_grad = (
        jnp.einsum("hij,ihc->jhc", score_grad, queries, preferred_element_type=jnp.float32)
        .astype(jnp.bfloat16)
        .reshape(rows, -1)
    )
    values_grad = values_grad.reshape(rows, -1)
    table_grad = jnp.dot(
        lookup.T, diagonal_sums(score_grad.astype(jnp.float32)).T, precision=lax.Precision.HIGHEST
    )
    query_grad = jnp.einsum("td,tc->dc", normed, queries_grad, preferred_element_type=jnp.float32)
    key_grad = jnp.einsum("td,tc->dc", normed, keys_grad, preferred_element_type=jnp.float32)
    value_grad = jnp.einsum("td,tc->dc", normed, values_grad, preferred_element_type=jnp.float32)
    normed_part = (
        jnp.einsum("tc,dc->td", queries_grad, query_weight, preferred_element_type=jnp.float32)
        + jnp.einsum("tc,dc->td", keys_grad, key_weight, preferred_element_type=jnp.float32)
        + jnp.einsum("tc,dc->td", values_grad, value_weight, preferred_element_type=jnp.float32)
    )
    normed_grad = pair_sum(normed_part.astype(jnp.bfloat16), 1)
    input_part_grad, attn_gain_grad = rms_back(inputs, attn_gain, scale_one, normed_grad)
    tokens_grad = (middle_grad + input_part_grad).astype(jnp.bfloat16)
    wide, thin = reduce_grads(
        query_grad,
        key_grad,
        value_grad,
        output_weight_grad,
        [attn_gain_grad, table_grad, ffn_gain_grad, router_grad],
        experts,
        quarter,
    )
    summed = (
        thin[0],
        wide[0],
        wide[1],
        wide[2],
        wide[3],
        thin[1],
        thin[2],
        thin[3],
    )
    return (
        output,
        tokens_grad,
        summed[0],
        summed[1],
        summed[2],
        summed[3],
        summed[4],
        summed[5],
        summed[6],
        summed[7],
        expert_in_grad,
        expert_out_grad,
    )


def solution(mesh):
    return jax.shard_map(
        local,
        mesh=mesh,
        in_specs=(
            P("dp", None),
            P("dp", None),
            P(),
            P(),
            P("dp", None),
            P(),
            P(),
            P(None, "tensor"),
            P(None, "tensor"),
            P(None, "tensor"),
            P("tensor", None),
            P(None, "tensor"),
            P(),
            P(),
            P(None, ("dp", "tensor")),
            P(("dp", "tensor"), None),
        ),
        out_specs=(
            P("dp", None),
            P("dp", None),
            P(),
            P(None, "tensor"),
            P(None, "tensor"),
            P(None, "tensor"),
            P("tensor", None),
            P(None, "tensor"),
            P(),
            P(),
            P(None, ("dp", "tensor")),
            P(("dp", "tensor"), None),
        ),
        check_vma=False,
    )
```
